128 devices in a mesh: dp: 2 (over y_lo), out: 16 (over x, z), in: 4 (over y_hi, core).
Axes of the slice: x: 4, y: 4 (y_hi: 2, y_lo: 2; y = y_hi * 2 + y_lo), z: 4, core: 2. Of those that a mesh axis runs over, the one named last changes fastest.
Arguments:
- features: bfloat16 [3072, 6144], P('dp', 'in'), may hold values from -6 to 6
- grad_qkv: bfloat16 [3072, 18432], P(('dp', 'in'), 'out'), may hold values from -0.47851562 to 0.47851562
- grad_act: bfloat16 [3072, 24576], P(('dp', 'in'), 'out'), may hold values from -0.47851562 to 0.47851562
- preact: bfloat16 [3072, 24576], P(('dp', 'in'), 'out'), may hold values from -9 to 9
- w_qkv: bfloat16 [6144, 18432], P('in', 'out'), may hold values from -0.078125 to 0.078125
- w_mlp: bfloat16 [6144, 24576], P('in', 'out'), may hold values from -0.078125 to 0.078125
Outputs:
- grad_features: bfloat16 [3072, 6144], P(('dp', 'out'), 'in')
- grad_wqkv: bfloat16 [6144, 18432], P('in', 'out')
- grad_wmlp: bfloat16 [6144, 24576], P('in', 'out')
The draws below stay inside these ranges and needn't reach their ends.
All inputs are finite; a program needn't handle non-finite values.
Results may differ from the reference program's by a relative error of at most 0.0059.
Values may be sent and summed in bfloat16 or wider, within the bound.
A program may use at most 128 MiB of HBM per device.

```python
import math
import jax
import jax.numpy as jnp
from jax import lax

D = 6144
FF = 24576
TOK_DEV = 1536
TOKENS = 3072
N_DP = 2


def shard_levels(stream_key, extent, cuts, low, high):
    gain = 1.0
    for dim, parts in cuts:
        steps = jax.random.uniform(jax.random.fold_in(jax.random.fold_in(stream_key, 6), dim), (parts,), jnp.float32, low / len(cuts), high / len(cuts))
        gain = gain * jnp.repeat(jnp.exp(steps), extent[dim] // parts).reshape((-1,) + (1,) * (len(extent) - 1 - dim))
    return gain


def noise(own_key, extent, width, most, cuts=(), held_as=jnp.bfloat16):
    values = width * jax.random.normal(own_key, extent, jnp.float32)
    if cuts:
        values = values * shard_levels(own_key, extent, cuts, -0.22, 0.18)
    return jnp.clip(values, -most, most).astype(held_as)


def setup_inputs(seed: int = 0) -> dict:
    seeds = jax.random.split(jax.random.key(seed), 7)
    return {
        "features": noise(seeds[0], (TOKENS, D), 1.0, 6.0, ((0, 2), (1, 4))),
        "grad_qkv": noise(seeds[1], (TOKENS, 3 * D), 0.08, 0.47851562, ((0, 8), (1, 16))),
        "grad_act": noise(seeds[2], (TOKENS, FF), 0.08, 0.47851562, ((0, 8), (1, 16))),
        "preact": noise(seeds[3], (TOKENS, FF), 1.5, 9.0, ((0, 8), (1, 16))),
        "w_qkv": noise(seeds[4], (D, 3 * D), D ** -0.5, 0.078125, ((0, 4), (1, 16))),
        "w_mlp": noise(seeds[5], (D, FF), D ** -0.5, 0.078125, ((0, 4), (1, 16))),
    }


def gelu_slope(values):
    cumulative = 0.5 * (1.0 + lax.erf(values / math.sqrt(2.0)))
    density = jnp.exp(-0.5 * values * values) / math.sqrt(2.0 * math.pi)
    return cumulative + values * density

def reference(features, grad_qkv, grad_act, preact, w_qkv, w_mlp):
    derivative = gelu_slope(preact.astype(jnp.float32))
    grad_hidden = (grad_act.astype(jnp.float32) * derivative).astype(jnp.bfloat16)
    qkv_term = lax.dot_general(grad_qkv, w_qkv, (((1,), (1,)), ((), ())), preferred_element_type=jnp.float32)
    mlp_term = lax.dot_general(grad_hidden, w_mlp, (((1,), (1,)), ((), ())), preferred_element_type=jnp.float32)
    grad_features = (qkv_term + mlp_term).astype(jnp.bfloat16)
    total_qkv = jnp.zeros(w_qkv.shape, jnp.float32)
    total_mlp = jnp.zeros(w_mlp.shape, jnp.float32)
    for replica in range(N_DP):
        first_row = replica * TOK_DEV
        block_feat = features[first_row:first_row + TOK_DEV]
        block_qkv = grad_qkv[first_row:first_row + TOK_DEV]
        block_mlp = grad_hidden[first_row:first_row + TOK_DEV]
        part_qkv = lax.dot_general(block_feat, block_qkv, (((0,), (0,)), ((), ())), preferred_element_type=jnp.float32)
        part_mlp = lax.dot_general(block_feat, block_mlp, (((0,), (0,)), ((), ())), preferred_element_type=jnp.float32)
        total_qkv = total_qkv + part_qkv.astype(jnp.bfloat16).astype(jnp.float32)
        total_mlp = total_mlp + part_mlp.astype(jnp.bfloat16).astype(jnp.float32)
    return (grad_features, total_qkv.astype(jnp.bfloat16), total_mlp.astype(jnp.bfloat16))
```

```python
import math

import jax
import jax.numpy as jnp
from jax import lax
from jax.experimental import pallas as pl
from jax.experimental.pallas import tpu as pltpu
from jax.sharding import PartitionSpec as P

MESH = pl.DeviceIdType.MESH
BF = jnp.bfloat16
F32 = jnp.float32
NQ, NM, F = 1152, 1536, 1536
COLS = ((0, 0, 512), (0, 512, 512), (0, 1024, 128), (1, 0, 512), (1, 512, 512), (1, 1024, 512))


def gelu_slope(values):
    cumulative = 0.5 * (1.0 + lax.erf(values * (1.0 / math.sqrt(2.0))))
    density = jnp.exp(-0.5 * values * values) * (1.0 / math.sqrt(2.0 * math.pi))
    return cumulative + values * density


def kernel(feat, gq, ga, pre, wq_hbm, wm_hbm, gf_out, oq_hbm, om_hbm,
           Gq, Gm, FT, FTo, Wq, Wm, Pp, ra, rb, rx1, rx2, piece, stg, gout, aq, am,
           ssem, rsem, lsem):
    dp, o, i = lax.axis_index("dp"), lax.axis_index("out"), lax.axis_index("in")
    hi, core = i // 2, i % 2
    x, z = o // 4, o % 4
    same = 1 - (dp + core) % 2
    hiA = same * hi + (1 - same) * (1 - hi)
    hiB = 1 - hiA
    p1 = (hiB + core) % 2
    devA = (1 - dp, o, 2 * hiA + core)
    devB = (1 - dp, o, 2 * hiB + core)
    sib = (dp, o, 2 * hi + 1 - core)
    partner = (1 - dp, o, i)

    def at(xx, zz):
        return ((xx + 4) % 4) * 4 + (zz + 4) % 4

    def plane(xx, zz):
        return (dp, at(xx, zz), i)

    G, W, ACC, OUT = (Gq, Gm), (Wq, Wm), (aq, am), (oq_hbm, om_hbm)

    ids = {}
    sent = []

    def rc(key, src, dst, dev):
        n = ids.setdefault(key, len(ids))
        return pltpu.make_async_remote_copy(src_ref=src, dst_ref=dst, send_sem=ssem.at[n], recv_sem=rsem.at[n],
                                            device_id=dev, device_id_type=MESH)

    def send(key, src, dst, dev, when=None):
        c = rc(key, src, dst, dev)
        if when is None:
            c.start()
        else:
            pl.when(when)(c.start)
        sent.append((c, when))

    def got(key, dst):
        rc(key, dst, dst, sib).wait_recv()

    lids = {}
    lwait = {}

    def local(key, src, dst):
        n = lids.setdefault(key, len(lids))
        c = pltpu.make_async_copy(src, dst, lsem.at[n])
        c.start()
        lwait[key] = c

    for c in range(3):
        local(("ga", c), ga.at[:, c], stg.at[0, c])
        local(("pre", c), pre.at[:, c], stg.at[1, c])
        if c == 0:
            for b in range(4):
                for cc in range(3):
                    local(("f", b, cc), feat.at[b, :, cc], Pp.at[b // 2, cc, b % 2])
    for c in range(3):
        local(("q", c), gq.at[:, c], Gq.at[0, c, core])
    local(("wq",), wq_hbm, Wq)
    local(("wm",), wm_hbm, Wm)

    bar = pltpu.get_barrier_semaphore()
    friends = (devA, devB, sib, plane(x + 1, z), plane(x - 1, z), plane(x, z + 1), plane(x, z - 1))
    for d in friends:
        pl.semaphore_signal(bar, inc=1, device_id=d, device_id_type=MESH)
    pl.semaphore_wait(bar, len(friends))

    def tok(k, slot, c, pos):
        return G[k].at[slot, c, pos]

    def own_q(c):
        send(("y1", 0, c), gq.at[:, c], tok(0, 1, c, hi), devA)
        send(("s0", 0, c), gq.at[:, c], tok(0, 0, c, core), sib)

    def own_m(c):
        lwait["ga", c].wait()
        lwait["pre", c].wait()

        def body(j, carry):
            a = stg[0, c, j].astype(F32)
            v = stg[1, c, j].astype(F32)
            Gm[0, c, core, j] = (a * gelu_slope(v)).astype(BF)
            return carry

        lax.fori_loop(0, 4, body, 0)
        send(("y1", 1, c), tok(1, 0, c, core), tok(1, 1, c, hi), devA)
        send(("s0", 1, c), tok(1, 0, c, core), tok(1, 0, c, core), sib)

    def Y1(c):
        for k in (0, 1):
            here = tok(k, 1, c, hiB)
            got(("y1", k, c), here)
            send(("y2", k, c), here, tok(k, 2, c, core), devA)
            send(("s1", k, c), here, here, sib)

    def Y2(c):
        for k in (0, 1):
            here = tok(k, 2, c, core)
            got(("y2", k, c), here)
            send(("s2", k, c), here, here, sib)

    def SIB(slot, c):
        pos = {0: 1 - core, 1: 1 - hiB, 2: 1 - core}[slot]
        for k in (0, 1):
            got(("s%d" % slot, k, c), tok(k, slot, c, pos))

    def col(n, slot, pos):
        k, c0, w = COLS[n]
        return G[k].at[slot, :, pos, :, :, pl.ds(c0, w)]

    def SEND3(n):
        send(("y3", n), col(n, 0, core), col(n, 3, hi), devB)

    def Y3(n):
        here = col(n, 3, hiA)
        got(("y3", n), here)
        send(("s3", n), here, here, sib)

    def SIB3(n):
        got(("s3", n), col(n, 3, 1 - hiA))

    def transpose():
        for b in range(4):
            for c in range(3):
                lwait["f", b, c].wait()
                h, p = b // 2, b % 2
                v = Pp[h, c, p].reshape(128, F)
                FT[h, :, c * 256 + p * 128:c * 256 + p * 128 + 128] = v.T
        rows = pl.ds(pl.multiple_of(o * 96, 32), 96)
        for b in range(4):
            h, p = b // 2, b % 2
            for c in range(3):
                piece[(h + p) % 2, :, c * 256 + h * 128:c * 256 + h * 128 + 128] = FT[h, rows, c * 256 + p * 128:c * 256 + p * 128 + 128]
        for p in (0, 1):
            send(("fp", p), piece.at[p], rows_of(p, o), partner)

    def rows_of(p, out, first=0, n=96):
        return FTo.at[p, pl.ds(pl.multiple_of(out * 96 + first, 16), n), :]

    def on(p, da, db):
        return at(x + da, z + db) if p == 0 else at(x + db, z + da)

    def to(p, da, db):
        return (dp, on(p, da, db), i)

    def F0():
        for p in (0, 1):
            here = rows_of(p, o)
            got(("fp", p), here)
            send(("f1", p, 0), here, here, to(p, 1, 0))
            send(("f1", p, 1), here, here, to(p, -1, 0))

    OFF = (0, -1, 1, 2)

    def spread(p, k):
        here = rows_of(p, on(p, OFF[k], 0))
        send(("f2", p, k, 0), here, here, to(p, 0, 1))
        send(("f2", p, k, 1), here, here, to(p, 0, -1))

    def F1():
        for p in (0, 1):
            got(("f1", p, 0), rows_of(p, on(p, -1, 0)))
            half = rows_of(p, on(p, -1, 0), 0, 48)
            send(("f1", p, 2), half, half, to(p, 1, 0))
            got(("f1", p, 1), rows_of(p, on(p, 1, 0)))
            half = rows_of(p, on(p, 1, 0), 48, 48)
            send(("f1", p, 3), half, half, to(p, -1, 0))
        for k in (0, 1, 2):
            for p in (0, 1):
                spread(p, k)

    def F2():
        for p in (0, 1):
            got(("f1", p, 2), rows_of(p, on(p, 2, 0), 0, 48))
            got(("f1", p, 3), rows_of(p, on(p, 2, 0), 48, 48))
            spread(p, 3)

    def F3(k):
        for p in (0, 1):
            side = 0 if k < 2 else 1
            here = rows_of(p, on(p, OFF[k], -1 if side == 0 else 1))
            got(("f2", p, k, side), here)
            send(("f3", p, k), here, here, to(p, 0, 1 if side == 0 else -1))

    def F4():
        for p in (0, 1):
            for k in range(4):
                side = 1 if k < 2 else 0
                got(("f2", p, k, side), rows_of(p, on(p, OFF[k], -1 if side == 0 else 1)))
                got(("f3", p, k), rows_of(p, on(p, OFF[k], 2)))

    def GF(s, c):
        slot = 2 * s
        a = Gq[slot, c].reshape(256, NQ)
        b = Gm[slot, c].reshape(256, NM)
        r = lax.dot_general(a, Wq[...], (((1,), (1,)), ((), ())), preferred_element_type=F32)
        r = r + lax.dot_general(b, Wm[...], (((1,), (1,)), ((), ())), preferred_element_type=F32)
        Pp[s, c] = r.astype(BF).reshape(2, 4, 32, F)

    zl, zr, z2 = (z + 3) % 4, (z + 1) % 4, (z + 2) % 4
    A, B = pl.ds(0, 768), pl.ds(768, 768)

    def role(s):
        h = hi if s == 0 else 1 - hi
        is_d = (x // 2) == h
        odd = x % 2
        keep = jnp.where(is_d, odd, 1 - odd)
        return is_d, odd, keep

    def R1(s, c):
        send(("r1", s, c, 0), Pp.at[s, c, :, z2, :, A], ra.at[s, c, 0], plane(x, z + 1))
        send(("r1", s, c, 1), Pp.at[s, c, :, z2, :, B], ra.at[s, c, 1], plane(x, z - 1))

    def R2(s, c):
        got(("r1", s, c, 0), ra.at[s, c, 0])
        Pp[s, c, :, zr, :, 0:768] = (Pp[s, c, :, zr, :, 0:768].astype(F32) + ra[s, c, 0].astype(F32)).astype(BF)
        send(("r2", s, c, 0), Pp.at[s, c, :, zr], rb.at[s, c, 0], plane(x, z + 1))
        got(("r1", s, c, 1), ra.at[s, c, 1])
        Pp[s, c, :, zl, :, 768:1536] = (Pp[s, c, :, zl, :, 768:1536].astype(F32) + ra[s, c, 1].astype(F32)).astype(BF)
        send(("r2", s, c, 1), Pp.at[s, c, :, zl], rb.at[s, c, 1], plane(x, z - 1))

    def R3(s, c):
        is_d, odd, keep = role(s)
        got(("r2", s, c, 0), rb.at[s, c, 0])
        got(("r2", s, c, 1), rb.at[s, c, 1])
        v = Pp[s, c, :, z].astype(F32) + rb[s, c, 0].astype(F32) + rb[s, c, 1].astype(F32)
        Pp[s, c, :, z] = v.astype(BF)
        send(("r3", s, c), Pp.at[s, c, 1 - keep, z], rx1.at[s, c], plane(x + 1 - 2 * odd, z))

    def R4(s, c):
        is_d, odd, keep = role(s)
        got(("r3", s, c), rx1.at[s, c])
        Pp[s, c, keep, z] = (Pp[s, c, keep, z].astype(F32) + rx1[s, c].astype(F32)).astype(BF)
        send(("r4", s, c), Pp.at[s, c, keep, z], rx2.at[s, c], plane(x - 1 + 2 * odd, z), when=jnp.logical_not(is_d))

    def R5(s, c):
        is_d, odd, keep = role(s)

        @pl.when(is_d)
        def _():
            got(("r4", s, c), rx2.at[s, c])
            gout[c] = (Pp[s, c, keep, z].astype(F32) + rx2[s, c].astype(F32)).astype(BF)

    def PASS(slot, n):
        k, c0, w = COLS[n]
        f = (FT.at[hi], FTo.at[p1], FT.at[1 - hi], FTo.at[1 - p1])[slot]
        acc = ACC[k]
        step = min(w, 256)

        def body(j, carry):
            cs = pl.ds(pl.multiple_of(c0 + j * step, 128), step)
            g = G[k][slot, :, :, :, :, cs].reshape(768, step)
            r = jnp.dot(f[...], g, preferred_element_type=F32)
            if slot == 0:
                acc[:, cs] = r
            elif slot < 3:
                acc[:, cs] += r
            else:
                W[k][:, cs] = (acc[:, cs] + r).astype(BF)
            return carry

        lax.fori_loop(0, w // step, body, 0)
        if slot == 3:
            local(("o", n), W[k].at[:, pl.ds(c0, w)], OUT[k].at[:, pl.ds(c0, w)])

    own_q(0)
    own_m(0)
    own_q(1)
    transpose()
    own_m(1)
    own_q(2)
    own_m(2)
    for c in range(3):
        lwait["q", c].wait()
    lwait["wq",].wait()
    lwait["wm",].wait()
    SIB(0, 0)
    GF(0, 0)
    F0()
    Y1(0)
    SIB(0, 1)
    GF(0, 1)
    F1()
    SIB(0, 2)
    GF(0, 2)
    F2()
    PASS(0, 0)
    Y1(1)
    R1(0, 0)
    PASS(0, 1)
    PASS(0, 2)
    F3(0)
    R1(0, 1)
    PASS(0, 3)
    R2(0, 0)
    F3(1)
    PASS(0, 4)
    F3(2)
    R1(0, 2)
    R2(0, 1)
    PASS(0, 5)
    Y1(2)
    F3(3)
    R3(0, 0)
    R2(0, 2)
    Y2(0)
    R3(0, 1)
    R4(0, 0)
    SIB(2, 0)
    GF(1, 0)
    R1(1, 0)
    R3(0, 2)
    R4(0, 1)
    R5(0, 0)
    SEND3(0)
    Y2(1)
    R4(0, 2)
    R5(0, 1)
    SIB(2, 1)
    GF(1, 1)
    R1(1, 1)
    R2(1, 0)
    SEND3(1)
    SEND3(2)
    R5(0, 2)
    Y2(2)
    for n in (3, 4, 5):
        SEND3(n)
    SIB(2, 2)
    GF(1, 2)
    R1(1, 2)
    R2(1, 1)
    R3(1, 0)
    PASS(2, 0)
    PASS(2, 1)
    R2(1, 2)
    R3(1, 1)
    R4(1, 0)
    PASS(2, 2)
    PASS(2, 3)
    R3(1, 2)
    R4(1, 1)
    R5(1, 0)
    Y3(0)
    PASS(2, 4)
    PASS(2, 5)
    R4(1, 2)
    R5(1, 1)
    Y3(1)
    F4()
    for c in range(3):
        SIB(1, c)
    PASS(1, 0)
    R5(1, 2)
    for c in range(3):
        local(("gf", c), gout.at[c], gf_out.at[c])
    PASS(1, 1)
    Y3(2)
    PASS(1, 2)
    PASS(1, 3)
    Y3(3)
    PASS(1, 4)
    PASS(1, 5)
    for n in range(6):
        if n >= 4:
            Y3(n)
        SIB3(n)
        PASS(3, n)
    for n in range(6):
        lwait["o", n].wait()
    for c in range(3):
        lwait["gf", c].wait()
    for c, when in sent:
        if when is None:
            c.wait_send()
        else:
            pl.when(when)(c.wait_send)


def local(features, grad_qkv, grad_act, preact, w_qkv, w_mlp):
    shape = jax.ShapeDtypeStruct
    vm = pltpu.VMEM
    gf, gwq, gwm = pl.pallas_call(
        kernel,
        name="joined_projection_backward",
        out_shape=(shape((3, 32, F), BF), shape((F, NQ), BF), shape((F, NM), BF)),
        in_specs=[pl.BlockSpec(memory_space=pl.ANY)] * 6,
        out_specs=(pl.BlockSpec(memory_space=pl.ANY),) * 3,
        scratch_shapes=[
            vm((4, 3, 2, 4, 32, NQ), BF),
            vm((4, 3, 2, 4, 32, NM), BF),
            vm((2, F, 768), BF),
            vm((2, F, 768), BF),
            vm((F, NQ), BF),
            vm((F, NM), BF),
            vm((2, 3, 2, 4, 32, F), BF),
            vm((2, 3, 2, 2, 32, 768), BF),
            vm((2, 3, 2, 2, 32, F), BF),
            vm((2, 3, 32, F), BF),
            vm((2, 3, 32, F), BF),
            vm((2, 96, 768), BF),
            vm((2, 3, 4, 32, NM), BF),
            vm((3, 32, F), BF),
            vm((F, NQ), F32),
            vm((F, NM), F32),
            pltpu.SemaphoreType.DMA((112,)),
            pltpu.SemaphoreType.DMA((112,)),
            pltpu.SemaphoreType.DMA((32,)),
        ],
        compiler_params=pltpu.CompilerParams(collective_id=0, has_side_effects=True, vmem_limit_bytes=64 * 2**20 - 2**16),
        cost_estimate=pl.CostEstimate(flops=38_000_000_000, bytes_accessed=25_000_000, transcendentals=1_200_000),
    )(
        features.reshape(4, 4, 3, 32, F),
        grad_qkv.reshape(4, 3, 32, NQ),
        grad_act.reshape(4, 3, 32, NM),
        preact.reshape(4, 3, 32, NM),
        w_qkv,
        w_mlp,
    )
    return gf.reshape(96, F), gwq, gwm


def solution(mesh):
    return jax.shard_map(
        local,
        mesh=mesh,
        in_specs=(
            P("dp", "in"),
            P(("dp", "in"), "out"),
            P(("dp", "in"), "out"),
            P(("dp", "in"), "out"),
            P("in", "out"),
            P("in", "out"),
        ),
        out_specs=(P(("dp", "out"), "in"), P("in", "out"), P("in", "out")),
        check_vma=False,
    )
```

```python
import math

import jax
import jax.numpy as jnp
from jax import lax
from jax.experimental import pallas as pl
from jax.experimental.pallas import tpu as pltpu
from jax.sharding import PartitionSpec as P

MESH = pl.DeviceIdType.MESH
BF = jnp.bfloat16
F32 = jnp.float32
NQ, NM, F = 1152, 1536, 1536
COLS = ((0, 0, 512), (0, 512, 512), (0, 1024, 128), (1, 0, 512), (1, 512, 512), (1, 1024, 512))


def gelu_slope(values):
    cumulative = 0.5 * (1.0 + lax.erf(values * (1.0 / math.sqrt(2.0))))
    density = jnp.exp(-0.5 * values * values) * (1.0 / math.sqrt(2.0 * math.pi))
    return cumulative + values * density


def kernel(feat, gq, ga, pre, wq_hbm, wm_hbm, gf_out, oq_hbm, om_hbm,
           Gq, Gm, FT, FTo, Wq, Wm, Pp, ra, rb, rx1, rx2, piece, stg, gout, aq, am,
           ssem, rsem, lsem):
    dp, o, i = lax.axis_index("dp"), lax.axis_index("out"), lax.axis_index("in")
    hi, core = i // 2, i % 2
    x, z = o // 4, o % 4
    same = 1 - (dp + core) % 2
    hiA = same * hi + (1 - same) * (1 - hi)
    hiB = 1 - hiA
    p1 = (hiB + core) % 2
    devA = (1 - dp, o, 2 * hiA + core)
    devB = (1 - dp, o, 2 * hiB + core)
    sib = (dp, o, 2 * hi + 1 - core)
    partner = (1 - dp, o, i)

    def at(xx, zz):
        return ((xx + 4) % 4) * 4 + (zz + 4) % 4

    def plane(xx, zz):
        return (dp, at(xx, zz), i)

    G, W, ACC, OUT = (Gq, Gm), (Wq, Wm), (aq, am), (oq_hbm, om_hbm)

    ids = {}
    sent = []

    def rc(key, src, dst, dev):
        n = ids.setdefault(key, len(ids))
        return pltpu.make_async_remote_copy(src_ref=src, dst_ref=dst, send_sem=ssem.at[n], recv_sem=rsem.at[n],
                                            device_id=dev, device_id_type=MESH)

    def send(key, src, dst, dev, when=None):
        c = rc(key, src, dst, dev)
        if when is None:
            c.start()
        else:
            pl.when(when)(c.start)
        sent.append((c, when))

    def got(key, dst):
        rc(key, dst, dst, sib).wait_recv()

    lids = {}
    lwait = {}

    def local(key, src, dst):
        n = lids.setdefault(key, len(lids))
        c = pltpu.make_async_copy(src, dst, lsem.at[n])
        c.start()
        lwait[key] = c

    for b in range(4):
        for c in range(3):
            local(("f", b, c), feat.at[b, :, c], Pp.at[b // 2, c, b % 2])
    for c in range(3):
        local(("ga", c), ga.at[:, c], stg.at[0, c])
        local(("pre", c), pre.at[:, c], stg.at[1, c])
    for c in range(3):
        local(("q", c), gq.at[:, c], Gq.at[0, c, core])
    local(("wq",), wq_hbm, Wq)
    local(("wm",), wm_hbm, Wm)

    bar = pltpu.get_barrier_semaphore()
    friends = (devA, devB, sib, plane(x + 1, z), plane(x - 1, z), plane(x, z + 1), plane(x, z - 1))
    for d in friends:
        pl.semaphore_signal(bar, inc=1, device_id=d, device_id_type=MESH)

    def friends_here():
        pl.semaphore_wait(bar, len(friends))

    def tok(k, slot, c, pos):
        return G[k].at[slot, c, pos]

    def own(c):
        send(("y1", 0, c), gq.at[:, c], tok(0, 1, c, hi), devA)
        send(("y1", 1, c), tok(1, 0, c, core), tok(1, 1, c, hi), devA)

    def sib_q(c):
        send(("s0", 0, c), gq.at[:, c], tok(0, 0, c, core), sib)

    def slope(c):
        lwait["ga", c].wait()
        lwait["pre", c].wait()

        def body(j, carry):
            a = stg[0, c, j].astype(F32)
            v = stg[1, c, j].astype(F32)
            Gm[0, c, core, j] = (a * gelu_slope(v)).astype(BF)
            return carry

        lax.fori_loop(0, 4, body, 0)

    def sib_m(c):
        send(("s0", 1, c), tok(1, 0, c, core), tok(1, 0, c, core), sib)

    def Y1(c):
        for k in (0, 1):
            here = tok(k, 1, c, hiB)
            got(("y1", k, c), here)
            send(("y2", k, c), here, tok(k, 2, c, core), devA)
            send(("s1", k, c), here, here, sib)

    def Y2(c):
        for k in (0, 1):
            here = tok(k, 2, c, core)
            got(("y2", k, c), here)
            send(("s2", k, c), here, here, sib)

    def SIB(slot, c):
        pos = {0: 1 - core, 1: 1 - hiB, 2: 1 - core}[slot]
        for k in (0, 1):
            got(("s%d" % slot, k, c), tok(k, slot, c, pos))

    def col(n, slot, pos):
        k, c0, w = COLS[n]
        return G[k].at[slot, :, pos, :, :, pl.ds(c0, w)]

    def SEND3(n, light=None):
        send(("y3", n), col(n, 0, core), col(n, 3, hi), devB, None if light is None else same == light)

    def DETOUR3(n):
        k, c0, w = COLS[n]
        light = same
        src = G[k].at[2 - 2 * light, :, core, :, :, pl.ds(c0, w)]
        origin = light * hi + (1 - light) * (1 - hi)
        dev = (1 - dp, o, 2 * (light * hiB + (1 - light) * hiA) + core)
        send(("y3", n), src, G[k].at[3, :, origin, :, :, pl.ds(c0, w)], dev)

    def Y3(n):
        here = col(n, 3, hiA)
        got(("y3", n), here)
        send(("s3", n), here, here, sib)

    def SIB3(n):
        got(("s3", n), col(n, 3, 1 - hiA))

    def transpose():
        for b in range(4):
            for c in range(3):
                lwait["f", b, c].wait()
                h, p = b // 2, b % 2
                v = Pp[h, c, p].reshape(128, F)
                FT[h, :, c * 256 + p * 128:c * 256 + p * 128 + 128] = v.T
        rows = pl.ds(pl.multiple_of(o * 96, 32), 96)
        for b in range(4):
            h, p = b // 2, b % 2
            for c in range(3):
                piece[(h + p) % 2, :, c * 256 + h * 128:c * 256 + h * 128 + 128] = FT[h, rows, c * 256 + p * 128:c * 256 + p * 128 + 128]

    def pair(j):
        return p1 if j == 0 else 1 - p1

    def pieces(j):
        p = 1 - pair(j)
        send(("fp", j), piece.at[p], rows_of(p, o), partner)

    def rows_of(p, out, first=0, n=96):
        return FTo.at[p, pl.ds(pl.multiple_of(out * 96 + first, 16), n), :]

    def rows_at(j, dz, dx, first=0, n=96):
        return rows_of(pair(j), at(x + dx, z + dz), first, n)

    def F0(j):
        here = rows_at(j, 0, 0)
        got(("fp", j), here)
        send(("f1", j, 0), here, here, plane(x, z + 1))
        send(("f1", j, 1), here, here, plane(x, z - 1))

    OFF = (0, -1, 1, 2)

    def spread(j, k):
        here = rows_at(j, OFF[k], 0)
        send(("f2", j, k, 0), here, here, plane(x + 1, z))
        send(("f2", j, k, 1), here, here, plane(x - 1, z))

    def F1(j):
        got(("f1", j, 0), rows_at(j, -1, 0))
        half = rows_at(j, -1, 0, 0, 48)
        send(("f1", j, 2), half, half, plane(x, z + 1))
        got(("f1", j, 1), rows_at(j, 1, 0))
        half = rows_at(j, 1, 0, 48, 48)
        send(("f1", j, 3), half, half, plane(x, z - 1))

    def F2(j):
        got(("f1", j, 2), rows_at(j, 2, 0, 0, 48))
        got(("f1", j, 3), rows_at(j, 2, 0, 48, 48))
        spread(j, 3)

    def F3(j, k):
        side = 0 if k < 2 else 1
        here = rows_at(j, OFF[k], -1 if side == 0 else 1)
        got(("f2", j, k, side), here)
        send(("f3", j, k), here, here, plane(x + (1 if side == 0 else -1), z))

    def F4(j):
        for k in range(4):
            side = 1 if k < 2 else 0
            got(("f2", j, k, side), rows_at(j, OFF[k], -1 if side == 0 else 1))
            got(("f3", j, k), rows_at(j, OFF[k], 2))

    def GF(s, c):
        slot = 2 * s
        a = Gq[slot, c].reshape(256, NQ)
        b = Gm[slot, c].reshape(256, NM)
        r = lax.dot_general(a, Wq[...], (((1,), (1,)), ((), ())), preferred_element_type=F32)
        r = r + lax.dot_general(b, Wm[...], (((1,), (1,)), ((), ())), preferred_element_type=F32)
        Pp[s, c] = r.astype(BF).reshape(2, 4, 32, F)

    zl, zr, z2 = (z + 3) % 4, (z + 1) % 4, (z + 2) % 4
    A, B = pl.ds(0, 768), pl.ds(768, 768)

    def role(s):
        h = hi if s == 0 else 1 - hi
        is_d = (x // 2) == h
        odd = x % 2
        keep = jnp.where(is_d, odd, 1 - odd)
        return is_d, odd, keep

    def R1(s, c):
        send(("r1", s, c, 0), Pp.at[s, c, :, z2, :, A], ra.at[s, c, 0], plane(x, z + 1))
        send(("r1", s, c, 1), Pp.at[s, c, :, z2, :, B], ra.at[s, c, 1], plane(x, z - 1))

    def R2(s, c):
        got(("r1", s, c, 0), ra.at[s, c, 0])
        Pp[s, c, :, zr, :, 0:768] = (Pp[s, c, :, zr, :, 0:768].astype(F32) + ra[s, c, 0].astype(F32)).astype(BF)
        send(("r2", s, c, 0), Pp.at[s, c, :, zr], rb.at[s, c, 0], plane(x, z + 1))
        got(("r1", s, c, 1), ra.at[s, c, 1])
        Pp[s, c, :, zl, :, 768:1536] = (Pp[s, c, :, zl, :, 768:1536].astype(F32) + ra[s, c, 1].astype(F32)).astype(BF)
        send(("r2", s, c, 1), Pp.at[s, c, :, zl], rb.at[s, c, 1], plane(x, z - 1))

    def R3(s, c):
        is_d, odd, keep = role(s)
        got(("r2", s, c, 0), rb.at[s, c, 0])
        got(("r2", s, c, 1), rb.at[s, c, 1])
        v = Pp[s, c, :, z].astype(F32) + rb[s, c, 0].astype(F32) + rb[s, c, 1].astype(F32)
        Pp[s, c, :, z] = v.astype(BF)
        send(("r3", s, c), Pp.at[s, c, 1 - keep, z], rx1.at[s, c], plane(x + 1 - 2 * odd, z))

    def R4(s, c):
        is_d, odd, keep = role(s)
        got(("r3", s, c), rx1.at[s, c])
        Pp[s, c, keep, z] = (Pp[s, c, keep, z].astype(F32) + rx1[s, c].astype(F32)).astype(BF)
        send(("r4", s, c), Pp.at[s, c, keep, z], rx2.at[s, c], plane(x - 1 + 2 * odd, z), when=jnp.logical_not(is_d))

    def R5(s, c):
        is_d, odd, keep = role(s)

        @pl.when(is_d)
        def _():
            got(("r4", s, c), rx2.at[s, c])
            gout[c] = (Pp[s, c, keep, z].astype(F32) + rx2[s, c].astype(F32)).astype(BF)

    def PASS(slot, n, c0=0, c1=3):
        k, first, w = COLS[n]
        f = (FT.at[hi], FTo.at[p1], FT.at[1 - hi], FTo.at[1 - p1])[slot]
        acc = ACC[k]
        cs = pl.ds(first, w)
        g = G[k][slot, c0:c1, :, :, :, cs].reshape((c1 - c0) * 256, w)
        half = F if w > 256 else F // 2
        for m in range(0, F, half):
            ms = pl.ds(m, half)
            r = jnp.dot(f[ms, c0 * 256:c1 * 256], g, preferred_element_type=F32)
            if slot == 0:
                acc[ms, cs] = r
            elif slot < 3:
                acc[ms, cs] += r
            else:
                W[k][ms, cs] = (acc[ms, cs] + r).astype(BF)
        if slot == 3:
            local(("o", n), W[k].at[:, cs], OUT[k].at[:, cs])

    def result():
        for c in range(3):
            local(("gf", c), gout.at[c], gf_out.at[c])

    def loaded():
        for c in range(3):
            lwait["q", c].wait()
        lwait["wq",].wait()
        lwait["wm",].wait()

    transpose()
    slope(0)
    friends_here()
    pieces(0)
    pieces(1)
    own(0)
    sib_q(0)
    sib_m(0)
    sib_q(1)
    sib_q(2)
    slope(1)
    sib_m(1)
    slope(2)
    sib_m(2)
    loaded()
    SIB(0, 0)
    GF(0, 0)
    own(1)
    SIB(0, 1)
    GF(0, 1)
    F0(0)
    spread(0, 0)
    SIB(0, 2)
    GF(0, 2)
    own(2)
    PASS(0, 0)
    F1(0)
    spread(0, 1)
    spread(0, 2)
    F0(1)
    PASS(0, 1)
    PASS(0, 2)
    PASS(0, 3)
    F2(0)
    Y1(0)
    PASS(0, 4)
    F1(1)
    PASS(0, 5)
    R1(0, 0)
    R1(0, 1)
    R1(0, 2)
    F3(0, 0)
    F3(0, 1)
    Y1(1)
    F3(0, 2)
    F3(0, 3)
    R2(0, 0)
    Y1(2)
    spread(1, 0)
    R2(0, 1)
    spread(1, 1)
    R2(0, 2)
    spread(1, 2)
    F2(1)
    SIB(1, 0)
    SIB(1, 1)
    SIB(1, 2)
    F4(0)
    PASS(1, 0)
    PASS(1, 1)
    Y2(0)
    PASS(1, 2)
    SIB(2, 0)
    GF(1, 0)
    R1(1, 0)
    F3(1, 0)
    R3(0, 0)
    PASS(1, 3)
    Y2(1)
    SEND3(0, 1)
    SEND3(1, 1)
    PASS(1, 4)
    SIB(2, 1)
    GF(1, 1)
    R1(1, 1)
    R2(1, 0)
    F3(1, 1)
    R3(0, 1)
    PASS(1, 5)
    F3(1, 2)
    Y2(2)
    SEND3(0, 0)
    SEND3(1, 0)
    SEND3(2)
    SEND3(3)
    PASS(2, 0, 0, 2)
    SIB(2, 2)
    GF(1, 2)
    R1(1, 2)
    R2(1, 1)
    SEND3(4)
    DETOUR3(5)
    F3(1, 3)
    PASS(2, 1, 0, 2)
    Y3(0)
    R3(1, 0)
    PASS(2, 2, 0, 2)
    PASS(2, 3, 0, 2)
    R3(0, 2)
    R4(0, 0)
    Y3(1)
    PASS(2, 4, 0, 2)
    PASS(2, 5, 0, 2)
    R2(1, 2)
    Y3(2)
    PASS(2, 0, 2, 3)
    PASS(2, 1, 2, 3)
    PASS(2, 2, 2, 3)
    R4(1, 0)
    PASS(2, 3, 2, 3)
    PASS(2, 4, 2, 3)
    R4(0, 1)
    PASS(2, 5, 2, 3)
    R3(1, 1)
    F4(1)
    SIB3(0)
    PASS(3, 0)
    Y3(3)
    SIB3(1)
    PASS(3, 1)
    SIB3(2)
    PASS(3, 2)
    R3(1, 2)
    R4(1, 1)
    R4(0, 2)
    R5(0, 0)
    SIB3(3)
    PASS(3, 3)
    Y3(4)
    R5(0, 1)
    R5(1, 0)
    SIB3(4)
    PASS(3, 4)
    R4(1, 2)
    Y3(5)
    R5(1, 1)
    R5(0, 2)
    SIB3(5)
    PASS(3, 5)
    R5(1, 2)
    result()
    for n in range(6):
        lwait["o", n].wait()
    for c in range(3):
        lwait["gf", c].wait()
    for c, when in sent:
        if when is None:
            c.wait_send()
        else:
            pl.when(when)(c.wait_send)


def copy_out(a, b, c, x, y, z, va, vb, vc, sem):
    parts = []
    for src, mid, dst, n in ((b, vb, y, 4), (c, vc, z, 4), (a, va, x, 1)):
        rows = src.shape[0] // n
        for j in range(n):
            r = pl.ds(j * rows, rows)
            i = len(parts)
            parts.append((pltpu.make_async_copy(src.at[r], mid.at[r], sem.at[0, i]), pltpu.make_async_copy(mid.at[r], dst.at[r], sem.at[1, i])))
    for load, _ in parts:
        load.start()
    for load, store in parts:
        load.wait()
        store.start()
    for _, store in parts:
        store.wait()


def local(features, grad_qkv, grad_act, preact, w_qkv, w_mlp):
    shape = jax.ShapeDtypeStruct
    vm = pltpu.VMEM
    gf, gwq, gwm = pl.pallas_call(
        kernel,
        name="joined_projection_backward",
        out_shape=(shape((3, 32, F), BF), shape((F, NQ), BF), shape((F, NM), BF)),
        in_specs=[pl.BlockSpec(memory_space=pl.ANY)] * 6,
        out_specs=(pl.BlockSpec(memory_space=pl.ANY),) * 3,
        scratch_shapes=[
            vm((4, 3, 2, 4, 32, NQ), BF),
            vm((4, 3, 2, 4, 32, NM), BF),
            vm((2, F, 768), BF),
            vm((2, F, 768), BF),
            vm((F, NQ), BF),
            vm((F, NM), BF),
            vm((2, 3, 2, 4, 32, F), BF),
            vm((2, 3, 2, 2, 32, 768), BF),
            vm((2, 3, 2, 2, 32, F), BF),
            vm((2, 3, 32, F), BF),
            vm((2, 3, 32, F), BF),
            vm((2, 96, 768), BF),
            vm((2, 3, 4, 32, NM), BF),
            vm((3, 32, F), BF),
            vm((F, NQ), F32),
            vm((F, NM), F32),
            pltpu.SemaphoreType.DMA((112,)),
            pltpu.SemaphoreType.DMA((112,)),
            pltpu.SemaphoreType.DMA((32,)),
        ],
        compiler_params=pltpu.CompilerParams(collective_id=0, has_side_effects=True, vmem_limit_bytes=64 * 2**20 - 2**16),
        cost_estimate=pl.CostEstimate(flops=38_000_000_000, bytes_accessed=25_000_000, transcendentals=1_200_000),
    )(
        features.reshape(4, 4, 3, 32, F),
        grad_qkv.reshape(4, 3, 32, NQ),
        grad_act.reshape(4, 3, 32, NM),
        preact.reshape(4, 3, 32, NM),
        w_qkv,
        w_mlp,
    )
    gf = gf.reshape(96, F)
    return pl.pallas_call(
        copy_out,
        name="results",
        out_shape=tuple(shape(v.shape, BF) for v in (gf, gwq, gwm)),
        in_specs=[pl.BlockSpec(memory_space=pl.ANY)] * 3,
        out_specs=(pl.BlockSpec(memory_space=pl.ANY),) * 3,
        scratch_shapes=[vm(v.shape, BF) for v in (gf, gwq, gwm)] + [pltpu.SemaphoreType.DMA((2, 9))],
        compiler_params=pltpu.CompilerParams(vmem_limit_bytes=60 * 2**20),
        cost_estimate=pl.CostEstimate(flops=0, bytes_accessed=17_000_000, transcendentals=0),
    )(gf, gwq, gwm)


def solution(mesh):
    return jax.shard_map(
        local,
        mesh=mesh,
        in_specs=(
            P("dp", "in"),
            P(("dp", "in"), "out"),
            P(("dp", "in"), "out"),
            P(("dp", "in"), "out"),
            P("in", "out"),
            P("in", "out"),
        ),
        out_specs=(P(("dp", "out"), "in"), P("in", "out"), P("in", "out")),
        check_vma=False,
    )
```

```python
import math

import jax
import jax.numpy as jnp
from jax import lax
from jax.experimental import pallas as pl
from jax.experimental.pallas import tpu as pltpu
from jax.sharding import PartitionSpec as P

MESH = pl.DeviceIdType.MESH
BF = jnp.bfloat16
F32 = jnp.float32
NQ, NM, F = 1152, 1536, 1536
COLS = ((0, 0, 512), (0, 512, 512), (0, 1024, 128), (1, 0, 512), (1, 512, 512), (1, 1024, 512))


def gelu_slope(values):
    cumulative = 0.5 * (1.0 + lax.erf(values * (1.0 / math.sqrt(2.0))))
    density = jnp.exp(-0.5 * values * values) * (1.0 / math.sqrt(2.0 * math.pi))
    return cumulative + values * density


def kernel(feat, gq, ga, pre, wq_hbm, wm_hbm, gf_out, oq_hbm, om_hbm,
           Gq, Gm, FT, FTo, Wq, Wm, Pp, ra, rb, rx1, rx2, piece, stg, gout, aq, am,
           ssem, rsem, lsem):
    dp, o, i = lax.axis_index("dp"), lax.axis_index("out"), lax.axis_index("in")
    hi, core = i // 2, i % 2
    x, z = o // 4, o % 4
    same = 1 - (dp + core) % 2
    hiA = same * hi + (1 - same) * (1 - hi)
    hiB = 1 - hiA
    p1 = (hiB + core) % 2
    devA = (1 - dp, o, 2 * hiA + core)
    devB = (1 - dp, o, 2 * hiB + core)
    sib = (dp, o, 2 * hi + 1 - core)
    partner = (1 - dp, o, i)

    def at(xx, zz):
        return ((xx + 4) % 4) * 4 + (zz + 4) % 4

    def plane(xx, zz):
        return (dp, at(xx, zz), i)

    G, W, ACC, OUT = (Gq, Gm), (Wq, Wm), (aq, am), (oq_hbm, om_hbm)

    ids = {}
    sent = []

    def rc(key, src, dst, dev):
        n = ids.setdefault(key, len(ids))
        return pltpu.make_async_remote_copy(src_ref=src, dst_ref=dst, send_sem=ssem.at[n], recv_sem=rsem.at[n],
                                            device_id=dev, device_id_type=MESH)

    def send(key, src, dst, dev, when=None):
        c = rc(key, src, dst, dev)
        if when is None:
            c.start()
        else:
            pl.when(when)(c.start)
        sent.append((c, when))

    def got(key, dst):
        rc(key, dst, dst, sib).wait_recv()

    lids = {}
    lwait = {}

    def local(key, src, dst, after=None):
        n = lids[after] if after else lids.setdefault(key, len(lids))
        c = pltpu.make_async_copy(src, dst, lsem.at[n])
        c.start()
        lwait[key] = c

    for b in range(4):
        for c in range(3):
            local(("f", b, c), feat.at[b, :, c], Pp.at[b // 2, c, b % 2])
    for c in range(2):
        local(("ga", c), ga.at[:, c], stg.at[0, c])
        local(("pre", c), pre.at[:, c], stg.at[1, c])
    for c in range(3):
        local(("q", c), gq.at[:, c], Gq.at[0, c, core])
    local(("wq",), wq_hbm, Wq)
    local(("wm",), wm_hbm, Wm)

    bar = pltpu.get_barrier_semaphore()
    friends = (devA, devB, sib, plane(x + 1, z), plane(x - 1, z), plane(x, z + 1), plane(x, z - 1))
    for d in friends:
        pl.semaphore_signal(bar, inc=1, device_id=d, device_id_type=MESH)

    def friends_here():
        pl.semaphore_wait(bar, len(friends))

    def tok(k, slot, c, pos):
        return G[k].at[slot, c, pos]

    def own(c):
        send(("y1", 0, c), gq.at[:, c], tok(0, 1, c, hi), devA)
        send(("y1", 1, c), tok(1, 0, c, core), tok(1, 1, c, hi), devA)

    def sib_q(c):
        send(("s0", 0, c), gq.at[:, c], tok(0, 0, c, core), sib)

    def slope(c):
        lwait["ga", c].wait()
        lwait["pre", c].wait()

        def body(j, carry):
            a = stg[0, c % 2, j].astype(F32)
            v = stg[1, c % 2, j].astype(F32)
            Gm[0, c, core, j] = (a * gelu_slope(v)).astype(BF)
            return carry

        lax.fori_loop(0, 4, body, 0)
        if c == 0:
            local(("ga", 2), ga.at[:, 2], stg.at[0, 0], ("ga", 0))
            local(("pre", 2), pre.at[:, 2], stg.at[1, 0], ("pre", 0))

    def sib_m(c):
        send(("s0", 1, c), tok(1, 0, c, core), tok(1, 0, c, core), sib)

    def Y1(c):
        for k in (0, 1):
            here = tok(k, 1, c, hiB)
            got(("y1", k, c), here)
            send(("y2", k, c), here, tok(k, 2, c, core), devA)
            send(("s1", k, c), here, here, sib)

    def Y2(c):
        for k in (0, 1):
            here = tok(k, 2, c, core)
            got(("y2", k, c), here)
            send(("s2", k, c), here, here, sib)

    def SIB(slot, c):
        pos = {0: 1 - core, 1: 1 - hiB, 2: 1 - core}[slot]
        for k in (0, 1):
            got(("s%d" % slot, k, c), tok(k, slot, c, pos))

    def col(n, slot, pos):
        k, c0, w = COLS[n]
        return G[k].at[slot, :, pos, :, :, pl.ds(c0, w)]

    def SEND3(n, light=None):
        send(("y3", n), col(n, 0, core), col(n, 3, hi), devB, None if light is None else same == light)

    PARTS = (pl.ds(0, 2), pl.ds(2, 1))

    def part(n, j, slot, pos):
        k, c0, w = COLS[n]
        return G[k].at[slot, PARTS[j], pos, :, :, pl.ds(c0, w)]

    def DETOUR3(n):
        light = same
        origin = light * hi + (1 - light) * (1 - hi)
        dev = (1 - dp, o, 2 * (light * hiB + (1 - light) * hiA) + core)
        send(("y3", n, 0), part(n, 0, 2 - 2 * light, core), part(n, 0, 3, origin), dev)
        send(("y3", n, 1), part(n, 1, 0, core), part(n, 1, 3, hi), devB)

    def Y3(n):
        here = col(n, 3, hiA)
        if n == 5:
            for j in (0, 1):
                got(("y3", n, j), part(n, j, 3, hiA))
        else:
            got(("y3", n), here)
        send(("s3", n), here, here, sib)

    def SIB3(n):
        got(("s3", n), col(n, 3, 1 - hiA))

    def transpose():
        for b in range(4):
            for c in range(3):
                lwait["f", b, c].wait()
                h, p = b // 2, b % 2
                v = Pp[h, c, p].reshape(128, F)
                FT[h, :, c * 256 + p * 128:c * 256 + p * 128 + 128] = v.T
        rows = pl.ds(pl.multiple_of(o * 96, 32), 96)
        for b in range(4):
            h, p = b // 2, b % 2
            for c in range(3):
                piece[(h + p) % 2, :, c * 256 + h * 128:c * 256 + h * 128 + 128] = FT[h, rows, c * 256 + p * 128:c * 256 + p * 128 + 128]

    def pair(j):
        return p1 if j == 0 else 1 - p1

    def pieces(j):
        p = 1 - pair(j)
        send(("fp", j), piece.at[p], rows_of(p, o), partner)

    def rows_of(p, out, first=0, n=96):
        return FTo.at[p, pl.ds(pl.multiple_of(out * 96 + first, 16), n), :]

    def rows_at(j, dz, dx, first=0, n=96):
        return rows_of(pair(j), at(x + dx, z + dz), first, n)

    def F0(j):
        here = rows_at(j, 0, 0)
        got(("fp", j), here)
        send(("f1", j, 0), here, here, plane(x, z + 1))
        send(("f1", j, 1), here, here, plane(x, z - 1))

    OFF = (0, -1, 1, 2)

    def spread(j, k):
        here = rows_at(j, OFF[k], 0)
        send(("f2", j, k, 0), here, here, plane(x + 1, z))
        send(("f2", j, k, 1), here, here, plane(x - 1, z))

    def F1(j):
        got(("f1", j, 0), rows_at(j, -1, 0))
        half = rows_at(j, -1, 0, 0, 48)
        send(("f1", j, 2), half, half, plane(x, z + 1))
        got(("f1", j, 1), rows_at(j, 1, 0))
        half = rows_at(j, 1, 0, 48, 48)
        send(("f1", j, 3), half, half, plane(x, z - 1))

    def F2(j):
        got(("f1", j, 2), rows_at(j, 2, 0, 0, 48))
        got(("f1", j, 3), rows_at(j, 2, 0, 48, 48))
        spread(j, 3)

    def F3(j, k):
        side = 0 if k < 2 else 1
        here = rows_at(j, OFF[k], -1 if side == 0 else 1)
        got(("f2", j, k, side), here)
        send(("f3", j, k), here, here, plane(x + (1 if side == 0 else -1), z))

    def F4(j):
        for k in range(4):
            side = 1 if k < 2 else 0
            got(("f2", j, k, side), rows_at(j, OFF[k], -1 if side == 0 else 1))
            got(("f3", j, k), rows_at(j, OFF[k], 2))

    def GF(s, c):
        slot = 2 * s
        if s == 1:
            SIB(2, c)
        a = Gq[slot, c].reshape(256, NQ)
        b = Gm[slot, c].reshape(256, NM)
        r = lax.dot_general(a, Wq[...], (((1,), (1,)), ((), ())), preferred_element_type=F32)
        r = r + lax.dot_general(b, Wm[...], (((1,), (1,)), ((), ())), preferred_element_type=F32)
        Pp[s, c] = r.astype(BF).reshape(2, 4, 32, F)

    zl, zr, z2 = (z + 3) % 4, (z + 1) % 4, (z + 2) % 4
    A, B = pl.ds(0, 768), pl.ds(768, 768)

    def role(s):
        h = hi if s == 0 else 1 - hi
        is_d = (x // 2) == h
        odd = x % 2
        keep = jnp.where(is_d, odd, 1 - odd)
        return is_d, odd, keep

    def rows(j):
        return pl.ds(0, 32) if j is None else pl.ds(16 * j, 16)

    def R1(s, c, j=None):
        r = rows(j)
        send(("r1", s, c, j, 0), Pp.at[s, c, :, z2, r, A], ra.at[s, c, 0, :, r], plane(x, z + 1))
        send(("r1", s, c, j, 1), Pp.at[s, c, :, z2, r, B], ra.at[s, c, 1, :, r], plane(x, z - 1))

    def R2(s, c, j=None):
        r = rows(j)
        got(("r1", s, c, j, 0), ra.at[s, c, 0, :, r])
        Pp[s, c, :, zr, r, 0:768] = (Pp[s, c, :, zr, r, 0:768].astype(F32) + ra[s, c, 0, :, r].astype(F32)).astype(BF)
        send(("r2", s, c, j, 0), Pp.at[s, c, :, zr, r], rb.at[s, c, 0, :, r], plane(x, z + 1))
        got(("r1", s, c, j, 1), ra.at[s, c, 1, :, r])
        Pp[s, c, :, zl, r, 768:1536] = (Pp[s, c, :, zl, r, 768:1536].astype(F32) + ra[s, c, 1, :, r].astype(F32)).astype(BF)
        send(("r2", s, c, j, 1), Pp.at[s, c, :, zl, r], rb.at[s, c, 1, :, r], plane(x, z - 1))

    def R3(s, c, j=None):
        r = rows(j)
        is_d, odd, keep = role(s)
        got(("r2", s, c, j, 0), rb.at[s, c, 0, :, r])
        got(("r2", s, c, j, 1), rb.at[s, c, 1, :, r])
        v = Pp[s, c, :, z, r].astype(F32) + rb[s, c, 0, :, r].astype(F32) + rb[s, c, 1, :, r].astype(F32)
        Pp[s, c, :, z, r] = v.astype(BF)
        send(("r3", s, c, j), Pp.at[s, c, 1 - keep, z, r], rx1.at[s, c, r], plane(x + 1 - 2 * odd, z))

    def R4(s, c, j=None):
        r = rows(j)
        is_d, odd, keep = role(s)
        got(("r3", s, c, j), rx1.at[s, c, r])
        Pp[s, c, keep, z, r] = (Pp[s, c, keep, z, r].astype(F32) + rx1[s, c, r].astype(F32)).astype(BF)
        send(("r4", s, c, j), Pp.at[s, c, keep, z, r], rx2.at[s, c, r], plane(x - 1 + 2 * odd, z), when=jnp.logical_not(is_d))

    def R5(s, c, j=None):
        r = rows(j)
        is_d, odd, keep = role(s)

        @pl.when(is_d)
        def _():
            got(("r4", s, c, j), rx2.at[s, c, r])
            gout[c, r] = (Pp[s, c, keep, z, r].astype(F32) + rx2[s, c, r].astype(F32)).astype(BF)

    def PASS(slot, n, c0=0, c1=3):
        k, first, w = COLS[n]
        f = (FT.at[hi], FTo.at[p1], FT.at[1 - hi], FTo.at[1 - p1])[slot]
        acc = ACC[k]
        cs = pl.ds(first, w)
        g = G[k][slot, c0:c1, :, :, :, cs].reshape((c1 - c0) * 256, w)
        half = F if w > 256 else F // 2
        for m in range(0, F, half):
            ms = pl.ds(m, half)
            r = jnp.dot(f[ms, c0 * 256:c1 * 256], g, preferred_element_type=F32)
            if slot == 0:
                acc[ms, cs] = r
            elif slot < 3:
                acc[ms, cs] += r
            else:
                W[k][ms, cs] = (acc[ms, cs] + r).astype(BF)
        if slot == 3:
            local(("o", n), W[k].at[:, cs], OUT[k].at[:, cs], ("f", n // 3, n % 3))

    def PASSM(c0, c1):
        def body(n, carry):
            cs = pl.ds(pl.multiple_of(n * 512, 512), 512)
            g = Gm[2, c0:c1, :, :, :, cs].reshape((c1 - c0) * 256, 512)
            for m in (0, 768):
                ms = pl.ds(m, 768)
                am[ms, cs] += jnp.dot(FT[1 - hi, ms, c0 * 256:c1 * 256], g, preferred_element_type=F32)
            return carry

        lax.fori_loop(0, 3, body, 0)

    def result(c):
        local(("gf", c), gout.at[c], gf_out.at[c], ("f", 2, c))

    def loaded():
        for c in range(3):
            lwait["q", c].wait()
        lwait["wq",].wait()
        lwait["wm",].wait()

    transpose()
    slope(0)
    friends_here()
    pieces(0)
    pieces(1)
    own(0)
    sib_q(0)
    sib_m(0)
    sib_q(1)
    sib_q(2)
    slope(1)
    sib_m(1)
    slope(2)
    sib_m(2)
    loaded()
    SIB(0, 0)
    GF(0, 0)
    own(1)
    SIB(0, 1)
    GF(0, 1)
    F0(0)
    spread(0, 0)
    SIB(0, 2)
    GF(0, 2)
    own(2)
    PASS(0, 0)
    F1(0)
    spread(0, 1)
    spread(0, 2)
    F0(1)
    PASS(0, 1)
    PASS(0, 2)
    PASS(0, 3)
    F2(0)
    Y1(0)
    PASS(0, 4)
    F1(1)
    PASS(0, 5)
    R1(0, 0)
    R1(0, 1)
    R1(0, 2)
    F3(0, 0)
    F3(0, 1)
    Y1(1)
    F3(0, 2)
    F3(0, 3)
    R2(0, 0)
    Y1(2)
    spread(1, 0)
    R2(0, 1)
    spread(1, 1)
    R2(0, 2)
    spread(1, 2)
    F2(1)
    SIB(1, 0)
    SIB(1, 1)
    SIB(1, 2)
    F4(0)
    PASS(1, 0)
    PASS(1, 1)
    PASS(1, 2)
    PASS(1, 3)
    Y2(0)
    PASS(1, 4)
    GF(1, 0)
    R1(1, 0)
    F3(1, 0)
    R3(0, 0)
    SEND3(0, 1)
    PASS(1, 5)
    Y2(1)
    SEND3(1, 1)
    PASS(2, 0, 0, 1)
    PASS(2, 1, 0, 1)
    PASS(2, 2, 0, 1)
    GF(1, 1)
    R1(1, 1)
    R2(1, 0)
    F3(1, 1)
    R3(0, 1)
    PASSM(0, 1)
    F3(1, 2)
    SEND3(3, 1)
    Y2(2)
    SEND3(0, 0)
    SEND3(1, 0)
    SEND3(3, 0)
    SEND3(4)
    PASS(2, 0, 1, 2)
    PASS(2, 1, 1, 2)
    PASS(2, 2, 1, 2)
    GF(1, 2)
    R1(1, 2, 0)
    R1(1, 2, 1)
    R2(1, 1)
    DETOUR3(5)
    SEND3(2)
    F3(1, 3)
    R3(0, 2)
    PASSM(1, 3)
    Y3(0)
    R2(1, 2, 0)
    R3(1, 0)
    R4(0, 0)
    PASS(2, 0, 2, 3)
    R2(1, 2, 1)
    PASS(2, 1, 2, 3)
    PASS(2, 2, 2, 3)
    Y3(1)
    F4(1)
    SIB3(0)
    PASS(3, 0)
    SIB3(1)
    PASS(3, 1)
    R3(1, 1)
    R4(1, 0)
    R4(0, 1)
    Y3(3)
    R3(1, 2, 0)
    R5(0, 0)
    SIB3(3)
    PASS(3, 3)
    R3(1, 2, 1)
    Y3(4)
    R4(1, 1)
    R4(0, 2)
    R4(1, 2, 0)
    Y3(5)
    SIB3(4)
    PASS(3, 4)
    R4(1, 2, 1)
    R5(1, 0)
    R5(0, 1)
    Y3(2)
    SIB3(5)
    PASS(3, 5)
    R5(0, 2)
    result(0)
    R5(1, 1)
    result(1)
    SIB3(2)
    PASS(3, 2)
    R5(1, 2, 0)
    R5(1, 2, 1)
    result(2)
    for n in range(6):
        lwait["o", n].wait()
    for c in range(3):
        lwait["gf", c].wait()
    for c, when in sent:
        if when is None:
            c.wait_send()
        else:
            pl.when(when)(c.wait_send)


def copy_out(a, b, c, x, y, z, va, vb, vc, sem):
    parts = []
    for src, mid, dst, n in ((b, vb, y, 4), (c, vc, z, 4), (a, va, x, 1)):
        rows = src.shape[0] // n
        for j in range(n):
            r = pl.ds(j * rows, rows)
            i = len(parts)
            parts.append((pltpu.make_async_copy(src.at[r], mid.at[r], sem.at[0, i]), pltpu.make_async_copy(mid.at[r], dst.at[r], sem.at[1, i])))
    for load, _ in parts:
        load.start()
    for load, store in parts:
        load.wait()
        store.start()
    for _, store in parts:
        store.wait()


def local(features, grad_qkv, grad_act, preact, w_qkv, w_mlp):
    shape = jax.ShapeDtypeStruct
    vm = pltpu.VMEM
    gf, gwq, gwm = pl.pallas_call(
        kernel,
        name="joined_projection_backward",
        out_shape=(shape((3, 32, F), BF), shape((F, NQ), BF), shape((F, NM), BF)),
        in_specs=[pl.BlockSpec(memory_space=pl.ANY)] * 6,
        out_specs=(pl.BlockSpec(memory_space=pl.ANY),) * 3,
        scratch_shapes=[
            vm((4, 3, 2, 4, 32, NQ), BF),
            vm((4, 3, 2, 4, 32, NM), BF),
            vm((2, F, 768), BF),
            vm((2, F, 768), BF),
            vm((F, NQ), BF),
            vm((F, NM), BF),
            vm((2, 3, 2, 4, 32, F), BF),
            vm((2, 3, 2, 2, 32, 768), BF),
            vm((2, 3, 2, 2, 32, F), BF),
            vm((2, 3, 32, F), BF),
            vm((2, 3, 32, F), BF),
            vm((2, 96, 768), BF),
            vm((2, 2, 4, 32, NM), BF),
            vm((3, 32, F), BF),
            vm((F, NQ), F32),
            vm((F, NM), F32),
            pltpu.SemaphoreType.DMA((119,)),
            pltpu.SemaphoreType.DMA((119,)),
            pltpu.SemaphoreType.DMA((21,)),
        ],
        compiler_params=pltpu.CompilerParams(collective_id=0, has_side_effects=True, vmem_limit_bytes=64 * 2**20 - 2**16),
        cost_estimate=pl.CostEstimate(flops=38_000_000_000, bytes_accessed=25_000_000, transcendentals=1_200_000),
    )(
        features.reshape(4, 4, 3, 32, F),
        grad_qkv.reshape(4, 3, 32, NQ),
        grad_act.reshape(4, 3, 32, NM),
        preact.reshape(4, 3, 32, NM),
        w_qkv,
        w_mlp,
    )
    gf = gf.reshape(96, F)
    return pl.pallas_call(
        copy_out,
        name="results",
        out_shape=tuple(shape(v.shape, BF) for v in (gf, gwq, gwm)),
        in_specs=[pl.BlockSpec(memory_space=pl.ANY)] * 3,
        out_specs=(pl.BlockSpec(memory_space=pl.ANY),) * 3,
        scratch_shapes=[vm(v.shape, BF) for v in (gf, gwq, gwm)] + [pltpu.SemaphoreType.DMA((2, 9))],
        compiler_params=pltpu.CompilerParams(vmem_limit_bytes=60 * 2**20),
        cost_estimate=pl.CostEstimate(flops=0, bytes_accessed=17_000_000, transcendentals=0),
    )(gf, gwq, gwm)


def solution(mesh):
    return jax.shard_map(
        local,
        mesh=mesh,
        in_specs=(
            P("dp", "in"),
            P(("dp", "in"), "out"),
            P(("dp", "in"), "out"),
            P(("dp", "in"), "out"),
            P("in", "out"),
            P("in", "out"),
        ),
        out_specs=(P(("dp", "out"), "in"), P("in", "out"), P("in", "out")),
        check_vma=False,
    )
```

```python
import math

import jax
import jax.numpy as jnp
from jax import lax
from jax.experimental import pallas as pl
from jax.experimental.pallas import tpu as pltpu
from jax.sharding import PartitionSpec as P

MESH = pl.DeviceIdType.MESH
BF = jnp.bfloat16
F32 = jnp.float32
NQ, NM, F = 1152, 1536, 1536
COLS = ((0, 0, 512), (0, 512, 512), (0, 1024, 128), (1, 0, 512), (1, 512, 512), (1, 1024, 512))


def gelu_slope(values):
    cumulative = 0.5 * (1.0 + lax.erf(values * (1.0 / math.sqrt(2.0))))
    density = jnp.exp(-0.5 * values * values) * (1.0 / math.sqrt(2.0 * math.pi))
    return cumulative + values * density


def kernel(feat, gq, ga, pre, wq_hbm, wm_hbm, gf_out, oq_hbm, om_hbm,
           Gq, Gm, FT, FTo, Wq, Wm, Pp, ra, rb, rx1, rx2, piece, stg, gout, aq, am,
           ssem, rsem, lsem):
    dp, o, i = lax.axis_index("dp"), lax.axis_index("out"), lax.axis_index("in")
    hi, core = i // 2, i % 2
    x, z = o // 4, o % 4
    same = 1 - (dp + core) % 2
    hiA = same * hi + (1 - same) * (1 - hi)
    hiB = 1 - hiA
    p1 = (hiB + core) % 2
    devA = (1 - dp, o, 2 * hiA + core)
    devB = (1 - dp, o, 2 * hiB + core)
    sib = (dp, o, 2 * hi + 1 - core)
    partner = (1 - dp, o, i)

    def at(xx, zz):
        return ((xx + 4) % 4) * 4 + (zz + 4) % 4

    def plane(xx, zz):
        return (dp, at(xx, zz), i)

    G, W, ACC, OUT = (Gq, Gm), (Wq, Wm), (aq, am), (oq_hbm, om_hbm)

    ids = {}
    sent = []

    def rc(key, src, dst, dev):
        n = ids.setdefault(key, len(ids))
        return pltpu.make_async_remote_copy(src_ref=src, dst_ref=dst, send_sem=ssem.at[n], recv_sem=rsem.at[n],
                                            device_id=dev, device_id_type=MESH)

    def send(key, src, dst, dev, when=None):
        c = rc(key, src, dst, dev)
        if when is None:
            c.start()
        else:
            pl.when(when)(c.start)
        sent.append((c, when))

    def got(key, dst):
        rc(key, dst, dst, sib).wait_recv()

    lids = {}
    lwait = {}

    def local(key, src, dst, after=None):
        n = lids[after] if after else lids.setdefault(key, len(lids))
        c = pltpu.make_async_copy(src, dst, lsem.at[n])
        c.start()
        lwait[key] = c

    for b in range(4):
        for c in range(3):
            local(("f", b, c), feat.at[b, :, c], Pp.at[b // 2, c, b % 2])
    for c in range(2):
        local(("ga", c), ga.at[:, c], stg.at[0, c])
        local(("pre", c), pre.at[:, c], stg.at[1, c])
    for c in range(3):
        local(("q", c), gq.at[:, c], Gq.at[0, c, core])
    local(("wq",), wq_hbm, Wq)
    local(("wm",), wm_hbm, Wm)

    bar = pltpu.get_barrier_semaphore()
    friends = (devA, devB, sib, plane(x + 1, z), plane(x - 1, z), plane(x, z + 1), plane(x, z - 1))
    for d in friends:
        pl.semaphore_signal(bar, inc=1, device_id=d, device_id_type=MESH)

    def friends_here():
        pl.semaphore_wait(bar, len(friends))

    def tok(k, slot, c, pos):
        return G[k].at[slot, c, pos]

    def own(c):
        send(("y1", 0, c), gq.at[:, c], tok(0, 1, c, hi), devA)
        send(("y1", 1, c), tok(1, 0, c, core), tok(1, 1, c, hi), devA)

    def sib_q(c):
        send(("s0", 0, c), gq.at[:, c], tok(0, 0, c, core), sib)

    def slope(c):
        lwait["ga", c].wait()
        lwait["pre", c].wait()

        def body(j, carry):
            a = stg[0, c % 2, j].astype(F32)
            v = stg[1, c % 2, j].astype(F32)
            Gm[0, c, core, j] = (a * gelu_slope(v)).astype(BF)
            return carry

        lax.fori_loop(0, 4, body, 0)
        if c == 0:
            local(("ga", 2), ga.at[:, 2], stg.at[0, 0], ("ga", 0))
            local(("pre", 2), pre.at[:, 2], stg.at[1, 0], ("pre", 0))

    def sib_m(c):
        send(("s0", 1, c), tok(1, 0, c, core), tok(1, 0, c, core), sib)

    def Y1(c):
        for k in (0, 1):
            here = tok(k, 1, c, hiB)
            got(("y1", k, c), here)
            send(("y2", k, c), here, tok(k, 2, c, core), devA)
            send(("s1", k, c), here, here, sib)

    def Y2(c):
        for k in (0, 1):
            here = tok(k, 2, c, core)
            got(("y2", k, c), here)
            send(("s2", k, c), here, here, sib)

    def SIB(slot, c):
        pos = {0: 1 - core, 1: 1 - hiB, 2: 1 - core}[slot]
        for k in (0, 1):
            got(("s%d" % slot, k, c), tok(k, slot, c, pos))

    def col(n, slot, pos):
        k, c0, w = COLS[n]
        return G[k].at[slot, :, pos, :, :, pl.ds(c0, w)]

    def SEND3(n, light=None):
        send(("y3", n), col(n, 0, core), col(n, 3, hi), devB, None if light is None else same == light)

    PARTS = (pl.ds(0, 2), pl.ds(2, 1))

    def part(n, j, slot, pos):
        k, c0, w = COLS[n]
        return G[k].at[slot, PARTS[j], pos, :, :, pl.ds(c0, w)]

    def DETOUR3(n):
        light = same
        origin = light * hi + (1 - light) * (1 - hi)
        dev = (1 - dp, o, 2 * (light * hiB + (1 - light) * hiA) + core)
        send(("y3", n, 0), part(n, 0, 2 - 2 * light, core), part(n, 0, 3, origin), dev)
        send(("y3", n, 1), part(n, 1, 0, core), part(n, 1, 3, hi), devB)

    def Y3(n):
        here = col(n, 3, hiA)
        if n == 5:
            for j in (0, 1):
                got(("y3", n, j), part(n, j, 3, hiA))
        else:
            got(("y3", n), here)
        send(("s3", n), here, here, sib)

    def SIB3(n):
        got(("s3", n), col(n, 3, 1 - hiA))

    def transpose():
        for b in range(4):
            for c in range(3):
                lwait["f", b, c].wait()
                h, p = b // 2, b % 2
                v = Pp[h, c, p].reshape(128, F)
                FT[h, :, c * 256 + p * 128:c * 256 + p * 128 + 128] = v.T
        rows = pl.ds(pl.multiple_of(o * 96, 32), 96)
        for b in range(4):
            h, p = b // 2, b % 2
            for c in range(3):
                piece[(h + p) % 2, :, c * 256 + h * 128:c * 256 + h * 128 + 128] = FT[h, rows, c * 256 + p * 128:c * 256 + p * 128 + 128]

    def pair(j):
        return p1 if j == 0 else 1 - p1

    def pieces(j):
        p = 1 - pair(j)
        send(("fp", j), piece.at[p], rows_of(p, o), partner)

    def rows_of(p, out, first=0, n=96):
        return FTo.at[p, pl.ds(pl.multiple_of(out * 96 + first, 16), n), :]

    def rows_at(j, dz, dx, first=0, n=96):
        return rows_of(pair(j), at(x + dx, z + dz), first, n)

    def F0(j):
        here = rows_at(j, 0, 0)
        got(("fp", j), here)
        send(("f1", j, 0), here, here, plane(x, z + 1))
        send(("f1", j, 1), here, here, plane(x, z - 1))

    OFF = (0, -1, 1, 2)

    def spread(j, k):
        here = rows_at(j, OFF[k], 0)
        send(("f2", j, k, 0), here, here, plane(x + 1, z))
        send(("f2", j, k, 1), here, here, plane(x - 1, z))

    def F1(j):
        got(("f1", j, 0), rows_at(j, -1, 0))
        half = rows_at(j, -1, 0, 0, 48)
        send(("f1", j, 2), half, half, plane(x, z + 1))
        got(("f1", j, 1), rows_at(j, 1, 0))
        half = rows_at(j, 1, 0, 48, 48)
        send(("f1", j, 3), half, half, plane(x, z - 1))

    def F2(j):
        got(("f1", j, 2), rows_at(j, 2, 0, 0, 48))
        got(("f1", j, 3), rows_at(j, 2, 0, 48, 48))
        spread(j, 3)

    def F3(j, k):
        side = 0 if k < 2 else 1
        here = rows_at(j, OFF[k], -1 if side == 0 else 1)
        got(("f2", j, k, side), here)
        send(("f3", j, k), here, here, plane(x + (1 if side == 0 else -1), z))

    def F4(j):
        for k in range(4):
            side = 1 if k < 2 else 0
            got(("f2", j, k, side), rows_at(j, OFF[k], -1 if side == 0 else 1))
            got(("f3", j, k), rows_at(j, OFF[k], 2))

    def GF(s, c):
        slot = 2 * s
        if s == 1:
            SIB(2, c)
        a = Gq[slot, c].reshape(256, NQ)
        b = Gm[slot, c].reshape(256, NM)
        r = lax.dot_general(a, Wq[...], (((1,), (1,)), ((), ())), preferred_element_type=F32)
        r = r + lax.dot_general(b, Wm[...], (((1,), (1,)), ((), ())), preferred_element_type=F32)
        Pp[s, c] = r.astype(BF).reshape(2, 4, 32, F)

    zl, zr, z2 = (z + 3) % 4, (z + 1) % 4, (z + 2) % 4
    A, B = pl.ds(0, 768), pl.ds(768, 768)

    def role(s):
        h = hi if s == 0 else 1 - hi
        is_d = (x // 2) == h
        odd = x % 2
        keep = jnp.where(is_d, odd, 1 - odd)
        return is_d, odd, keep

    def rows(j):
        return pl.ds(0, 32) if j is None else pl.ds(16 * j, 16)

    def R1(s, c, j=None):
        r = rows(j)
        send(("r1", s, c, j, 0), Pp.at[s, c, :, z2, r, A], ra.at[s, c, 0, :, r], plane(x, z + 1))
        send(("r1", s, c, j, 1), Pp.at[s, c, :, z2, r, B], ra.at[s, c, 1, :, r], plane(x, z - 1))

    def R2(s, c, j=None):
        r = rows(j)
        got(("r1", s, c, j, 0), ra.at[s, c, 0, :, r])
        Pp[s, c, :, zr, r, 0:768] = (Pp[s, c, :, zr, r, 0:768].astype(F32) + ra[s, c, 0, :, r].astype(F32)).astype(BF)
        send(("r2", s, c, j, 0), Pp.at[s, c, :, zr, r], rb.at[s, c, 0, :, r], plane(x, z + 1))
        got(("r1", s, c, j, 1), ra.at[s, c, 1, :, r])
        Pp[s, c, :, zl, r, 768:1536] = (Pp[s, c, :, zl, r, 768:1536].astype(F32) + ra[s, c, 1, :, r].astype(F32)).astype(BF)
        send(("r2", s, c, j, 1), Pp.at[s, c, :, zl, r], rb.at[s, c, 1, :, r], plane(x, z - 1))

    def R3(s, c, j=None):
        r = rows(j)
        is_d, odd, keep = role(s)
        got(("r2", s, c, j, 0), rb.at[s, c, 0, :, r])
        got(("r2", s, c, j, 1), rb.at[s, c, 1, :, r])
        v = Pp[s, c, :, z, r].astype(F32) + rb[s, c, 0, :, r].astype(F32) + rb[s, c, 1, :, r].astype(F32)
        Pp[s, c, :, z, r] = v.astype(BF)
        send(("r3", s, c, j), Pp.at[s, c, 1 - keep, z, r], rx1.at[s, c, r], plane(x + 1 - 2 * odd, z))

    def R4(s, c, j=None):
        r = rows(j)
        is_d, odd, keep = role(s)
        got(("r3", s, c, j), rx1.at[s, c, r])
        Pp[s, c, keep, z, r] = (Pp[s, c, keep, z, r].astype(F32) + rx1[s, c, r].astype(F32)).astype(BF)
        send(("r4", s, c, j), Pp.at[s, c, keep, z, r], rx2.at[s, c, r], plane(x - 1 + 2 * odd, z), when=jnp.logical_not(is_d))

    def R5(s, c, j=None):
        r = rows(j)
        is_d, odd, keep = role(s)

        @pl.when(is_d)
        def _():
            got(("r4", s, c, j), rx2.at[s, c, r])
            gout[c, r] = (Pp[s, c, keep, z, r].astype(F32) + rx2[s, c, r].astype(F32)).astype(BF)

    def PASS(slot, n, c0=0, c1=3):
        k, first, w = COLS[n]
        f = (FT.at[hi], FTo.at[p1], FT.at[1 - hi], FTo.at[1 - p1])[slot]
        acc = ACC[k]
        cs = pl.ds(first, w)
        g = G[k][slot, c0:c1, :, :, :, cs].reshape((c1 - c0) * 256, w)
        half = F if w > 256 else F // 2
        for m in range(0, F, half):
            ms = pl.ds(m, half)
            r = jnp.dot(f[ms, c0 * 256:c1 * 256], g, preferred_element_type=F32)
            if slot == 0:
                acc[ms, cs] = r
            elif slot < 3:
                acc[ms, cs] += r
            else:
                W[k][ms, cs] = (acc[ms, cs] + r).astype(BF)
        if slot == 3:
            local(("o", n), W[k].at[:, cs], OUT[k].at[:, cs], ("f", n // 3, n % 3))

    def PASSM(c0, c1):
        def body(n, carry):
            cs = pl.ds(pl.multiple_of(n * 512, 512), 512)
            g = Gm[2, c0:c1, :, :, :, cs].reshape((c1 - c0) * 256, 512)
            for m in (0, 768):
                ms = pl.ds(m, 768)
                am[ms, cs] += jnp.dot(FT[1 - hi, ms, c0 * 256:c1 * 256], g, preferred_element_type=F32)
            return carry

        lax.fori_loop(0, 3, body, 0)

    def result(c):
        local(("gf", c), gout.at[c], gf_out.at[c], ("f", 2, c))

    def loaded():
        for c in range(3):
            lwait["q", c].wait()
        lwait["wq",].wait()
        lwait["wm",].wait()

    transpose()
    slope(0)
    friends_here()
    pieces(0)
    pieces(1)
    own(0)
    sib_q(0)
    sib_m(0)
    sib_q(1)
    sib_q(2)
    slope(1)
    sib_m(1)
    slope(2)
    sib_m(2)
    loaded()
    SIB(0, 0)
    GF(0, 0)
    own(1)
    SIB(0, 1)
    GF(0, 1)
    F0(0)
    spread(0, 0)
    SIB(0, 2)
    GF(0, 2)
    own(2)
    PASS(0, 0)
    F1(0)
    spread(0, 1)
    spread(0, 2)
    F0(1)
    PASS(0, 1)
    PASS(0, 2)
    PASS(0, 3)
    F2(0)
    Y1(0)
    PASS(0, 4)
    F1(1)
    PASS(0, 5)
    R1(0, 0)
    R1(0, 1)
    R1(0, 2)
    F3(0, 0)
    F3(0, 1)
    Y1(1)
    F3(0, 2)
    F3(0, 3)
    R2(0, 0)
    Y1(2)
    spread(1, 0)
    R2(0, 1)
    spread(1, 1)
    R2(0, 2)
    spread(1, 2)
    F2(1)
    SIB(1, 0)
    SIB(1, 1)
    SIB(1, 2)
    F4(0)
    PASS(1, 0)
    PASS(1, 1)
    PASS(1, 2)
    PASS(1, 3)
    Y2(0)
    PASS(1, 4)
    GF(1, 0)
    R1(1, 0)
    F3(1, 0)
    R3(0, 0)
    SEND3(0, 1)
    PASS(1, 5)
    Y2(1)
    SEND3(1, 1)
    PASS(2, 0, 0, 1)
    PASS(2, 1, 0, 1)
    PASS(2, 2, 0, 1)
    GF(1, 1)
    R1(1, 1)
    R2(1, 0)
    F3(1, 1)
    R3(0, 1)
    PASSM(0, 1)
    F3(1, 2)
    SEND3(3, 1)
    Y2(2)
    SEND3(0, 0)
    SEND3(1, 0)
    SEND3(3, 0)
    SEND3(4)
    PASS(2, 0, 1, 2)
    PASS(2, 1, 1, 2)
    PASS(2, 2, 1, 2)
    GF(1, 2)
    R1(1, 2, 0)
    R1(1, 2, 1)
    R2(1, 1)
    DETOUR3(5)
    SEND3(2)
    F3(1, 3)
    R3(0, 2)
    PASSM(1, 3)
    Y3(0)
    R2(1, 2, 0)
    R3(1, 0)
    R4(0, 0)
    PASS(2, 0, 2, 3)
    R2(1, 2, 1)
    PASS(2, 1, 2, 3)
    PASS(2, 2, 2, 3)
    Y3(1)
    F4(1)
    SIB3(0)
    PASS(3, 0)
    SIB3(1)
    PASS(3, 1)
    R3(1, 1)
    R4(1, 0)
    R4(0, 1)
    Y3(3)
    R3(1, 2, 0)
    R5(0, 0)
    SIB3(3)
    PASS(3, 3)
    R3(1, 2, 1)
    Y3(4)
    R4(1, 1)
    R4(0, 2)
    R4(1, 2, 0)
    Y3(5)
    R4(1, 2, 1)
    SIB3(4)
    PASS(3, 4)
    R5(1, 0)
    R5(0, 1)
    Y3(2)
    SIB3(5)
    PASS(3, 5)
    R5(0, 2)
    result(0)
    R5(1, 1)
    result(1)
    SIB3(2)
    PASS(3, 2)
    R5(1, 2, 0)
    R5(1, 2, 1)
    result(2)
    for n in range(6):
        lwait["o", n].wait()
    for c in range(3):
        lwait["gf", c].wait()
    for c, when in sent:
        if when is None:
            c.wait_send()
        else:
            pl.when(when)(c.wait_send)


def copy_out(a, b, c, x, y, z, va, vb, vc, sem):
    parts = []
    for src, mid, dst, n in ((b, vb, y, 4), (c, vc, z, 4), (a, va, x, 1)):
        rows = src.shape[0] // n
        for j in range(n):
            r = pl.ds(j * rows, rows)
            i = len(parts)
            parts.append((pltpu.make_async_copy(src.at[r], mid.at[r], sem.at[0, i]), pltpu.make_async_copy(mid.at[r], dst.at[r], sem.at[1, i])))
    for load, _ in parts:
        load.start()
    for load, store in parts:
        load.wait()
        store.start()
    for _, store in parts:
        store.wait()


def local(features, grad_qkv, grad_act, preact, w_qkv, w_mlp):
    shape = jax.ShapeDtypeStruct
    vm = pltpu.VMEM
    gf, gwq, gwm = pl.pallas_call(
        kernel,
        name="joined_projection_backward",
        out_shape=(shape((3, 32, F), BF), shape((F, NQ), BF), shape((F, NM), BF)),
        in_specs=[pl.BlockSpec(memory_space=pl.ANY)] * 6,
        out_specs=(pl.BlockSpec(memory_space=pl.ANY),) * 3,
        scratch_shapes=[
            vm((4, 3, 2, 4, 32, NQ), BF),
            vm((4, 3, 2, 4, 32, NM), BF),
            vm((2, F, 768), BF),
            vm((2, F, 768), BF),
            vm((F, NQ), BF),
            vm((F, NM), BF),
            vm((2, 3, 2, 4, 32, F), BF),
            vm((2, 3, 2, 2, 32, 768), BF),
            vm((2, 3, 2, 2, 32, F), BF),
            vm((2, 3, 32, F), BF),
            vm((2, 3, 32, F), BF),
            vm((2, 96, 768), BF),
            vm((2, 2, 4, 32, NM), BF),
            vm((3, 32, F), BF),
            vm((F, NQ), F32),
            vm((F, NM), F32),
            pltpu.SemaphoreType.DMA((119,)),
            pltpu.SemaphoreType.DMA((119,)),
            pltpu.SemaphoreType.DMA((21,)),
        ],
        compiler_params=pltpu.CompilerParams(collective_id=0, has_side_effects=True, vmem_limit_bytes=64 * 2**20 - 2**16),
        cost_estimate=pl.CostEstimate(flops=38_000_000_000, bytes_accessed=25_000_000, transcendentals=1_200_000),
    )(
        features.reshape(4, 4, 3, 32, F),
        grad_qkv.reshape(4, 3, 32, NQ),
        grad_act.reshape(4, 3, 32, NM),
        preact.reshape(4, 3, 32, NM),
        w_qkv,
        w_mlp,
    )
    gf = gf.reshape(96, F)
    return pl.pallas_call(
        copy_out,
        name="results",
        out_shape=tuple(shape(v.shape, BF) for v in (gf, gwq, gwm)),
        in_specs=[pl.BlockSpec(memory_space=pl.ANY)] * 3,
        out_specs=(pl.BlockSpec(memory_space=pl.ANY),) * 3,
        scratch_shapes=[vm(v.shape, BF) for v in (gf, gwq, gwm)] + [pltpu.SemaphoreType.DMA((2, 9))],
        compiler_params=pltpu.CompilerParams(vmem_limit_bytes=60 * 2**20),
        cost_estimate=pl.CostEstimate(flops=0, bytes_accessed=17_000_000, transcendentals=0),
    )(gf, gwq, gwm)


def solution(mesh):
    return jax.shard_map(
        local,
        mesh=mesh,
        in_specs=(
            P("dp", "in"),
            P(("dp", "in"), "out"),
            P(("dp", "in"), "out"),
            P(("dp", "in"), "out"),
            P("in", "out"),
            P("in", "out"),
        ),
        out_specs=(P(("dp", "out"), "in"), P("in", "out"), P("in", "out")),
        check_vma=False,
    )
```
